128 devices in a mesh: ep: 32 (over x, z, core), hp: 4 (over y).
Axes of the slice: x: 4, y: 4, z: 4, core: 2. Of those that a mesh axis runs over, the one named last changes fastest.
Arguments:
- tokens: bfloat16 [8192, 4096], P('ep'), may hold values from -6 to 6
- expert_rows: int32 [64, 512], P('ep'), may hold values from 0 to 8191, as said below
- expert_counts: int32 [64], P('ep'), may hold values from 0 to 512, as said below
- choice_gates: float32 [64, 512], P('ep'), may hold values from 0.05 to 1
- gate_proj: bfloat16 [64, 4096, 1536], P('ep', None, 'hp'), may hold values from -0.09375 to 0.09375
- up_proj: bfloat16 [64, 4096, 1536], P('ep', None, 'hp'), may hold values from -0.09375 to 0.09375
- down_proj: bfloat16 [64, 1536, 4096], P('ep', 'hp'), may hold values from -0.15625 to 0.15625
Outputs:
- combined: bfloat16 [8192, 4096], P('ep', 'hp')
The draws below stay inside these ranges and needn't reach their ends.
Inputs may be any that keep to these rules, and one draw needn't show every extreme that they name: `expert_rows`: the first expert_counts[e] entries of row e are distinct tokens; later entries are padding and may name any token. Among the valid entries of one expert at most 16 lie in the 256 tokens of one index of ep, and in every draw some expert has exactly 16 from every index of ep. `expert_counts`: some expert's count is exactly 512 in every draw.
All inputs are finite; a program needn't handle non-finite values.
Results may differ from the reference program's by a relative error of at most 0.0049.
Values may be sent and summed in bfloat16 or wider, within the bound.
A program may use at most 128 MiB of HBM per device.

```python
import math
import jax
import jax.numpy as jnp
from jax import lax

D = 4096
H = 1536
TOK_DEV = 256
SLOT = 16
EXPERTS = 64
TOKENS = 8192
CAP = 512


def draw_lists(key):
    base = jax.random.fold_in(key, 7)
    key_count, key_full, key_perm, key_order, key_pad = jax.random.split(base, 5)
    sources = TOKENS // TOK_DEV
    per_pair = jax.random.randint(key_count, (EXPERTS, sources), 0, SLOT + 1)
    full_one = jax.random.randint(key_full, (), 0, EXPERTS)
    per_pair = jnp.where(jnp.arange(EXPERTS)[:, None] == full_one, SLOT, per_pair)
    perm_keys = jax.random.split(key_perm, EXPERTS * sources)

    def local_pick(subkey):
        return jax.random.permutation(subkey, TOK_DEV)[:SLOT]
    local_ids = jax.vmap(local_pick)(perm_keys).reshape(EXPERTS, sources, SLOT)
    global_ids = local_ids + (jnp.arange(sources) * TOK_DEV)[None, :, None]
    is_live = (jnp.arange(SLOT)[None, None, :] < per_pair[:, :, None]).reshape(EXPERTS, CAP)
    scores = jax.random.randint(key_order, (EXPERTS, CAP), 0, 2 ** 14) * CAP + jnp.arange(CAP)[None, :]
    scores = jnp.where(is_live, scores, scores + 2 ** 24)
    order = jnp.argsort(scores, axis=1)
    listed = jnp.take_along_axis(global_ids.reshape(EXPERTS, CAP), order, axis=1)
    counts = jnp.sum(per_pair, axis=1)
    padding = jax.random.randint(key_pad, (EXPERTS, CAP), 0, TOKENS)
    row_ids = jnp.where(jnp.arange(CAP)[None, :] < counts[:, None], listed, padding)
    return (row_ids.astype(jnp.int32), counts.astype(jnp.int32))


def draw_expert_rows(key, part):
    return draw_lists(key)[0]


def draw_expert_counts(key, part):
    return draw_lists(key)[1]


def block_scale(rng, extent, pieces, least, high):
    level = 1.0
    for position, blocks in pieces:
        draws = jax.random.uniform(jax.random.fold_in(jax.random.fold_in(rng, 6), position), (blocks,), jnp.float32, least / len(pieces), high / len(pieces))
        level = level * jnp.repeat(jnp.exp(draws), extent[position] // blocks).reshape((-1,) + (1,) * (len(extent) - 1 - position))
    return level


def bell_draw(key, shape, spread, reach, shards=(), held_as=jnp.bfloat16):
    loudness = block_scale(key, shape, shards, -0.22, 0.18) if shards else 1.0
    entries = jax.random.normal(key, shape, jnp.float32) * spread * loudness
    return jnp.minimum(jnp.maximum(entries, -reach), reach).astype(held_as)


def setup_inputs(seed: int = 0) -> dict:
    splits = jax.random.split(jax.random.key(seed), 8)
    tokens = bell_draw(splits[0], (TOKENS, D), 1.0, 6.0, ((0, 32),))
    expert_rows = draw_expert_rows(jax.random.fold_in(splits[7], 71), 0)
    expert_counts = draw_expert_counts(jax.random.fold_in(splits[7], 71), 0)
    choice_gates = jnp.clip(jnp.exp(math.log(1.0) - 2.9957323 * jax.random.uniform(splits[3], (EXPERTS, CAP), jnp.float32) ** block_scale(splits[3], (EXPERTS, CAP), ((0, 32),), -0.2, 0.2)), 0.05, 1.0)
    gate_proj = bell_draw(splits[4], (EXPERTS, D, H), D ** -0.5, 0.09375, ((0, 32), (2, 4)))
    up_proj = bell_draw(splits[5], (EXPERTS, D, H), D ** -0.5, 0.09375, ((0, 32), (2, 4)))
    down_proj = bell_draw(splits[6], (EXPERTS, H, D), H ** -0.5, 0.15625, ((0, 32), (1, 4)))
    return dict(tokens=tokens, expert_rows=expert_rows, expert_counts=expert_counts, choice_gates=choice_gates, gate_proj=gate_proj, up_proj=up_proj, down_proj=down_proj)


def reference(tokens, expert_rows, expert_counts, choice_gates, gate_proj, up_proj, down_proj):
    slots = jnp.arange(CAP, dtype=jnp.int32)

    def one_expert(total, per_expert):
        row_ids, live_count, gate_row, gate_mat, up_mat, down_mat = per_expert
        chosen = jnp.take(tokens, row_ids, axis=0).astype(jnp.float32)
        gate_act = jnp.dot(chosen, gate_mat.astype(jnp.float32), preferred_element_type=jnp.float32)
        up_act = jnp.dot(chosen, up_mat.astype(jnp.float32), preferred_element_type=jnp.float32)
        hidden = (jax.nn.silu(gate_act) * up_act).astype(jnp.bfloat16)
        expert_out = jnp.dot(hidden.astype(jnp.float32), down_mat.astype(jnp.float32), preferred_element_type=jnp.float32)
        weight = jnp.where(slots < live_count, gate_row, jnp.zeros_like(gate_row))
        return total.at[row_ids].add(expert_out * weight[:, None]), None

    start_total = jnp.zeros((TOKENS, D), jnp.float32)
    total, unused = lax.scan(one_expert, start_total, (expert_rows, expert_counts, choice_gates, gate_proj, up_proj, down_proj))
    return total.astype(jnp.bfloat16)
```

```python
import functools

import jax
import jax.numpy as jnp
from jax import lax
from jax.experimental import pallas as pl
from jax.experimental.pallas import tpu as pltpu
from jax.sharding import PartitionSpec as P

MESH = pl.DeviceIdType.MESH
SLOT = 16
BF16, F32, I32 = jnp.bfloat16, jnp.float32, jnp.int32


def plan(groups):
    side = {32: 4, 8: 2}[groups]
    ring = [min(d, side - d) for d in range(side)]
    chips = sorted(
        ((dx, dz) for dx in range(side) for dz in range(side)),
        key=lambda c: (side > 2 and 2 in c, ring[c[0]] + ring[c[1]], c[0] != c[1], c),
    )
    offsets = [(dx, dz, dc) for dx, dz in chips for dc in range(2)]
    if groups == 32:
        chunks = {
            "z": (0, 2, True), "a": (2, 10, True), "b": (10, 18, True), "d": (18, 22, True),
            "t": (22, 28, False), "s": (28, 32, False),
        }
        sends = "sztbda"
        schedule = (
            "XsXzXtCzEzGsXbGt",
            "AzBzTzFsFtXdCsEs",
            "XaCtEtAsBsCbEbAt",
            "BtTsCdEdTtAbBbCa",
            "EaAdBdTbAaBaTdMs",
            "MtMbTaMzMdMa",
        )
    else:
        chunks = {"a": (0, 4, True), "s": (4, 8, False)}
        sends = "sa"
        schedule = ("XsXaGsCaFs", "EaAaBaCs", "EsTaAsBsTs", "MaMs")
    steps = [(part[i], part[i + 1]) for part in schedule for i in range(0, len(part), 2)]
    return side, offsets, chunks, sends, steps


def kernel(
    groups, lanes_hp,
    rows_ref, counts_ref, gates_ref, tok_hbm, gate_hbm, up_hbm, down_hbm,
    out_ref,
    tok, wgu, wd, chosen, pout, via, fin, back, ret, onehot, acc, picks_out, picks_in, gate_col,
    w_sem, pick_s, pick_r, disp_s, disp_r, ret_s, ret_r, y_s, y_r,
):
    side, offsets, chunks, sends, schedule = plan(groups)
    places = groups
    n_exp, cap = rows_ref.shape
    n_q, n_tok, feat = tok.shape
    hid = wd.shape[2]
    me = lax.axis_index("ep")
    y = lax.axis_index("hp")
    mx, mz, mc = me // (side * 2), (me // 2) % side, me % 2
    y_up, y_dn, y_far = (y + 1) % n_q, (y + n_q - 1) % n_q, (y + 2) % n_q

    def shifted(p, sign):
        dx, dz, dc = offsets[p]
        px = (mx + (sign * dx) % side) % side
        pz = (mz + (sign * dz) % side) % side
        return (px * side + pz) * 2 + (mc + dc) % 2

    def expert_of(p):
        return {"ep": shifted(p, 1)}

    def owner_of(p):
        return {"ep": shifted(p, -1)}

    def remote(src, dst, s_sem, r_sem, device):
        return pltpu.make_async_remote_copy(
            src_ref=src, dst_ref=dst, send_sem=s_sem, recv_sem=r_sem,
            device_id=device, device_id_type=MESH,
        )

    loads = []

    def load(src, dst):
        copy = pltpu.make_async_copy(src, dst, w_sem.at[len(loads)])
        copy.start()
        loads.append(copy)

    for q in range(n_q):
        load(tok_hbm.at[:, pl.ds(q * feat, feat)], tok.at[q])
    for e in range(n_exp):
        load(gate_hbm.at[e], wgu.at[e, :, pl.ds(0, hid)])
        load(up_hbm.at[e], wgu.at[e, :, pl.ds(hid, hid)])
        for q in range(n_q):
            load(down_hbm.at[e, :, pl.ds(q * feat, feat)], wd.at[e, q])

    barrier = pltpu.get_barrier_semaphore()
    for p in range(1, places):
        pl.semaphore_signal(barrier, inc=1, device_id=expert_of(p), device_id_type=MESH)
    for target in (y_up, y_dn):
        pl.semaphore_signal(barrier, inc=1, device_id={"hp": target}, device_id_type=MESH)

    listed = rows_ref[...]
    entry = lax.broadcasted_iota(I32, (1, cap), 1)
    log_side = side.bit_length() - 1
    log_tok = n_tok.bit_length() - 1
    source = lax.shift_right_logical(listed, log_tok)
    row_in = listed & (n_tok - 1)
    sx = lax.shift_right_logical(source, log_side + 1)
    sz = lax.shift_right_logical(source, 1) & (side - 1)
    sc = source & 1
    code = (((mx - sx) & (side - 1)) * side + ((mz - sz) & (side - 1))) * 2 + ((mc - sc) & 1)
    place_code = [(dx * side + dz) * 2 + dc for dx, dz, dc in offsets]
    before = (
        lax.broadcasted_iota(I32, (cap, cap), 0) < lax.broadcasted_iota(I32, (cap, cap), 1)
    ).astype(F32).astype(BF16)
    place_id = lax.broadcasted_iota(I32, (places, 1), 0)
    place_codes = sum(jnp.where(place_id == p, c, 0) for p, c in enumerate(place_code))
    for e in range(n_exp):
        own_code = jnp.where(entry < counts_ref[e], code[e : e + 1, :], -1)
        hit = (own_code == place_codes).astype(F32)
        rank = jnp.dot(hit.astype(BF16), before, preferred_element_type=F32)
        slot = jnp.sum(
            hit * (rank + (lax.broadcasted_iota(I32, (places, cap), 0) * SLOT + 1).astype(F32)),
            axis=0, keepdims=True,
        ) - 1.0
        row_e = row_in[e : e + 1, :].astype(F32) + 1.0
        gate_e = gates_ref[e : e + 1, :]
        block = 4 * SLOT
        for b in range(places * SLOT // block):
            ids = (lax.broadcasted_iota(I32, (block, cap), 0) + b * block).astype(F32)
            here = ids == slot
            pick = jnp.sum(jnp.where(here, row_e, 0.0), axis=1, keepdims=True) - 1.0
            gate = jnp.sum(jnp.where(here, gate_e, 0.0), axis=1, keepdims=True)
            wide = jnp.broadcast_to(pick, (block, 128)).astype(BF16)
            picks_out[e, 4 * b : 4 * b + 4] = wide.reshape(4, SLOT, 128)
            gate_col[e, b * block : (b + 1) * block] = jnp.broadcast_to(gate, (block, 128))
    picks_in[:, 0] = picks_out[:, 0]

    pl.semaphore_wait(barrier, places - 1 + 2)

    order = [p for name in sends for p in range(*chunks[name][:2])]
    picks = {}
    for p in order:
        if p:
            picks[p] = remote(
                picks_out.at[:, p], picks_in.at[:, p], pick_s.at[p], pick_r.at[p], owner_of(p)
            )
            picks[p].start()

    for copy in loads[:n_q]:
        copy.wait()

    out_going = {}
    sem_ids = iter(range(y_s.shape[0]))
    started = []

    def send_y(src, dst, target):
        k = next(sem_ids)
        copy = remote(src, dst, y_s.at[k], y_r.at[k], {"hp": target})
        copy.start()
        started.append(copy)
        return copy

    state = {}
    returns = {}
    weights_ready = False

    for step, name in schedule:
        lo, hi, whole = chunks[name]
        n, m = hi - lo, (hi - lo) * SLOT
        rng = pl.ds(lo, n)
        if step == "X":
            for p in range(lo, hi):
                if p:
                    picks[p].wait_recv()
            token_id = lax.broadcasted_iota(I32, (m, 128), 1).astype(F32)
            for e in range(n_exp):
                want = picks_in[e, lo:hi].reshape(m, 128).astype(F32)
                parts = [
                    (token_id + float(128 * k) == want).astype(F32) for k in range(n_tok // 128)
                ]
                hot = jnp.concatenate(parts, axis=1).astype(BF16)
                onehot[e, lo:hi] = hot.reshape(n, SLOT, n_tok)

                def rows_of(q):
                    taken = jnp.dot(hot, tok[q], preferred_element_type=F32).astype(BF16)
                    pout[q, e, lo:hi] = taken.reshape(n, SLOT, feat)
                    if lo == 0:
                        chosen[q, e, 0] = taken[:SLOT]

                if whole:
                    pl.loop(0, n_q)(rows_of)
                else:
                    rows_of(y)
            for p in range(lo, hi):
                if p:
                    at = (slice(None), slice(None), p) if whole else (y, slice(None), p)
                    out_going[p] = remote(
                        pout.at[at], chosen.at[at], disp_s.at[p], disp_r.at[p], expert_of(p)
                    )
                    out_going[p].start()
        elif step == "G":
            for p in range(lo, hi):
                out_going[p].wait_recv()
            state[name, "G"] = [
                send_y(chosen.at[y, :, rng], chosen.at[y, :, rng], target) for target in (y_up, y_dn)
            ]
        elif step == "F":
            for copy in state[name, "G"]:
                copy.wait_recv()
            state[name, "F"] = [
                send_y(chosen.at[y_dn, 0, rng], chosen.at[y_dn, 0, rng], y_up),
                send_y(chosen.at[y_up, 1, rng], chosen.at[y_up, 1, rng], y_dn),
            ]
        elif step in "CE":
            e = "CE".index(step)
            if e == 0:
                for p in range(lo, hi):
                    if p and whole:
                        out_going[p].wait_recv()
                for p in range(lo, hi):
                    if p:
                        out_going[p].wait_send()
            if not weights_ready:
                for copy in loads[n_q:]:
                    copy.wait()
                weights_ready = True
            if not whole:
                state[name, "F"][e].wait_recv()
            total = jnp.zeros((m, 2 * hid), F32)
            for q in range(n_q):
                total += jnp.dot(
                    chosen[q, e, lo:hi].reshape(m, feat),
                    wgu[e, q * feat : (q + 1) * feat, :],
                    preferred_element_type=F32,
                )
            gate, up = total[:, :hid], total[:, hid:]
            hidden = (gate / (1.0 + jnp.exp(-gate)) * up).astype(BF16)
            weight = gate_col[e, lo * SLOT : hi * SLOT][:, :1]

            @pl.loop(0, n_q)
            def _(q):
                value = jnp.dot(hidden, wd[e, q], preferred_element_type=F32) * weight
                pout[q, e, lo:hi] = value.astype(BF16).reshape(n, SLOT, feat)

            ahead, behind = (y_up, y_dn) if e == 0 else (y_dn, y_up)
            state[name, "V", e] = send_y(pout.at[y_far, e, rng], via.at[e, rng], ahead)
            state[name, "D", e] = send_y(pout.at[behind, e, rng], fin.at[1 - e, e, rng], behind)
        elif step in "AB":
            e = "AB".index(step)
            ahead = (y_up, y_dn)[e]
            state[name, "V", e].wait_recv()
            pout[ahead, e, lo:hi] = (
                pout[ahead, e, lo:hi].astype(F32) + via[e, lo:hi].astype(F32)
            ).astype(BF16)
            state[name, "S", e] = send_y(pout.at[ahead, e, rng], fin.at[e, e, rng], ahead)
        elif step == "T":
            for e in range(n_exp):
                state[name, "D", e].wait_recv()
                state[name, "S", e].wait_recv()
                back[e, lo:hi] = (
                    pout[y, e, lo:hi].astype(F32)
                    + fin[0, e, lo:hi].astype(F32)
                    + fin[1, e, lo:hi].astype(F32)
                ).astype(BF16)
            for p in range(lo, hi):
                if p:
                    returns[p] = remote(
                        back.at[:, p], ret.at[:, p], ret_s.at[p], ret_r.at[p], owner_of(p)
                    )
                    returns[p].start()
                else:
                    ret[:, 0] = back[:, 0]
        else:
            for p in range(lo, hi):
                if p:
                    returns[p].wait_recv()
            total = None
            for e in range(n_exp):
                value = lax.dot_general(
                    onehot[e, lo:hi].reshape(m, n_tok),
                    ret[e, lo:hi].reshape(m, feat),
                    (((0,), (0,)), ((), ())),
                    preferred_element_type=F32,
                )
                total = value if total is None else total + value
            merged = [w for s, w in schedule if s == "M"]
            if name != merged[0]:
                total = total + acc[...]
            if name == merged[-1]:
                out_ref[...] = total.astype(BF16)
            else:
                acc[...] = total

    for copy in [*picks.values(), *returns.values(), *started]:
        copy.wait_send()


def per_device(tokens, expert_rows, expert_counts, choice_gates, gate_proj, up_proj, down_proj):
    groups = lax.axis_size("ep")
    n_q = lax.axis_size("hp")
    n_tok, width = tokens.shape
    n_exp, cap = expert_rows.shape
    hid = gate_proj.shape[2]
    feat = width // n_q
    chunks = plan(groups)[2]
    hops = sum(6 if whole else 10 for _, _, whole in chunks.values())
    any_space = pl.BlockSpec(memory_space=pl.ANY)
    vmem = pl.BlockSpec(memory_space=pltpu.VMEM)
    dma = pltpu.SemaphoreType.DMA
    full = (n_q, n_exp, groups, SLOT, feat)
    return pl.pallas_call(
        functools.partial(kernel, groups, n_q),
        out_shape=jax.ShapeDtypeStruct((n_tok, feat), BF16),
        in_specs=[vmem, pl.BlockSpec(memory_space=pltpu.SMEM), vmem, any_space, any_space, any_space, any_space],
        out_specs=vmem,
        scratch_shapes=[
            pltpu.VMEM((n_q, n_tok, feat), BF16),
            pltpu.VMEM((n_exp, width, 2 * hid), BF16),
            pltpu.VMEM((n_exp, n_q, hid, feat), BF16),
            pltpu.VMEM(full, BF16),
            pltpu.VMEM(full, BF16),
            pltpu.VMEM((2, groups, SLOT, feat), BF16),
            pltpu.VMEM((2, n_exp, groups, SLOT, feat), BF16),
            pltpu.VMEM((n_exp, groups, SLOT, feat), BF16),
            pltpu.VMEM((n_exp, groups, SLOT, feat), BF16),
            pltpu.VMEM((n_exp, groups, SLOT, n_tok), BF16),
            pltpu.VMEM((n_tok, feat), F32),
            pltpu.VMEM((n_exp, groups, SLOT, 128), BF16),
            pltpu.VMEM((n_exp, groups, SLOT, 128), BF16),
            pltpu.VMEM((n_exp, groups * SLOT, 128), F32),
            dma((n_q + n_exp * (2 + n_q),)),
            dma((groups,)),
            dma((groups,)),
            dma((groups,)),
            dma((groups,)),
            dma((groups,)),
            dma((groups,)),
            dma((hops,)),
            dma((hops,)),
        ],
        compiler_params=pltpu.CompilerParams(
            collective_id=0, has_side_effects=True, vmem_limit_bytes=60 * 1024 * 1024
        ),
        cost_estimate=pl.CostEstimate(
            flops=6 * n_exp * cap * width * hid, bytes_accessed=24 * 1024 * 1024, transcendentals=0
        ),
    )(
        expert_rows, expert_counts, choice_gates,
        tokens, gate_proj, up_proj, down_proj,
    )


def solution(mesh):
    return jax.shard_map(
        per_device,
        mesh=mesh,
        in_specs=(
            P("ep", None),
            P("ep", None),
            P("ep"),
            P("ep", None),
            P("ep", None, "hp"),
            P("ep", None, "hp"),
            P("ep", "hp", None),
        ),
        out_specs=P("ep", "hp"),
        check_vma=False,
    )
```

```python
import functools

import jax
import jax.numpy as jnp
from jax import lax
from jax.experimental import pallas as pl
from jax.experimental.pallas import tpu as pltpu
from jax.sharding import PartitionSpec as P

MESH = pl.DeviceIdType.MESH
SLOT = 16
BF16, F32, I32 = jnp.bfloat16, jnp.float32, jnp.int32


def plan(groups):
    side = {32: 4, 8: 2}[groups]
    ring = [min(d, side - d) for d in range(side)]
    chips = sorted(
        ((dx, dz) for dx in range(side) for dz in range(side)),
        key=lambda c: (side > 2 and 2 in c, ring[c[0]] + ring[c[1]], c[0] != c[1], c),
    )
    offsets = [(dx, dz, dc) for dx, dz in chips for dc in range(2)]
    if groups == 32:
        chunks = {
            "z": (0, 2, True), "a": (2, 6, True), "e": (6, 10, True), "b": (10, 18, True),
            "d": (18, 22, True), "t": (22, 28, False), "s": (28, 32, False),
        }
        sends = "sztbdae"
        schedule = (
            "XsXzXtCzEzGsXbAz",
            "BzGtFsXdFtCsEsXa",
            "XeTzCtEtAsBsCbEb",
            "AtBtTsCdEdTtAbBb",
            "CaEaAdBdTbCeEeAa",
            "BaTdAeBeTaMsMtMb",
            "TeMzMdMaMe",
        )
    else:
        chunks = {"a": (0, 4, True), "s": (4, 8, False)}
        sends = "sa"
        schedule = ("XsXaGsCaFs", "EaAaBaCs", "EsTaAsBsTs", "MaMs")
    steps = [(part[i], part[i + 1]) for part in schedule for i in range(0, len(part), 2)]
    return side, offsets, chunks, sends, steps


def kernel(
    groups, lanes_hp,
    rows_ref, counts_ref, gates_ref, tok_hbm, gate_hbm, up_hbm, down_hbm,
    out_ref,
    tok, wgu, wd, chosen, pout, via, fin, back, ret, onehot, acc, picks_out, picks_in, gate_col,
    w_sem, pick_s, pick_r, disp_s, disp_r, ret_s, ret_r, y_s, y_r,
):
    side, offsets, chunks, sends, schedule = plan(groups)
    places = groups
    n_exp, cap = rows_ref.shape
    n_q, n_tok, feat = tok.shape
    hid = wd.shape[2]
    me = lax.axis_index("ep")
    y = lax.axis_index("hp")
    mx, mz, mc = me // (side * 2), (me // 2) % side, me % 2
    y_up, y_dn, y_far = (y + 1) % n_q, (y + n_q - 1) % n_q, (y + 2) % n_q

    def shifted(p, sign):
        dx, dz, dc = offsets[p]
        px = (mx + (sign * dx) % side) % side
        pz = (mz + (sign * dz) % side) % side
        return (px * side + pz) * 2 + (mc + dc) % 2

    def expert_of(p):
        return {"ep": shifted(p, 1)}

    def owner_of(p):
        return {"ep": shifted(p, -1)}

    def remote(src, dst, s_sem, r_sem, device):
        return pltpu.make_async_remote_copy(
            src_ref=src, dst_ref=dst, send_sem=s_sem, recv_sem=r_sem,
            device_id=device, device_id_type=MESH,
        )

    loads = []

    def load(src, dst):
        copy = pltpu.make_async_copy(src, dst, w_sem.at[len(loads)])
        copy.start()
        loads.append(copy)

    for q in range(n_q):
        load(tok_hbm.at[:, pl.ds(q * feat, feat)], tok.at[q])
    for e in range(n_exp):
        load(gate_hbm.at[e], wgu.at[e, :, pl.ds(0, hid)])
        load(up_hbm.at[e], wgu.at[e, :, pl.ds(hid, hid)])
        for q in range(n_q):
            load(down_hbm.at[e, :, pl.ds(q * feat, feat)], wd.at[e, q])

    barrier = pltpu.get_barrier_semaphore()
    for p in range(1, places):
        pl.semaphore_signal(barrier, inc=1, device_id=expert_of(p), device_id_type=MESH)
    for target in (y_up, y_dn):
        pl.semaphore_signal(barrier, inc=1, device_id={"hp": target}, device_id_type=MESH)

    listed = rows_ref[...]
    entry = lax.broadcasted_iota(I32, (1, cap), 1)
    log_side = side.bit_length() - 1
    log_tok = n_tok.bit_length() - 1
    source = lax.shift_right_logical(listed, log_tok)
    row_in = listed & (n_tok - 1)
    sx = lax.shift_right_logical(source, log_side + 1)
    sz = lax.shift_right_logical(source, 1) & (side - 1)
    sc = source & 1
    code = (((mx - sx) & (side - 1)) * side + ((mz - sz) & (side - 1))) * 2 + ((mc - sc) & 1)
    place_code = [(dx * side + dz) * 2 + dc for dx, dz, dc in offsets]
    before = (
        lax.broadcasted_iota(I32, (cap, cap), 0) < lax.broadcasted_iota(I32, (cap, cap), 1)
    ).astype(F32).astype(BF16)
    place_id = lax.broadcasted_iota(I32, (places, 1), 0)
    place_codes = sum(jnp.where(place_id == p, c, 0) for p, c in enumerate(place_code))
    for e in range(n_exp):
        own_code = jnp.where(entry < counts_ref[e], code[e : e + 1, :], -1)
        hit = (own_code == place_codes).astype(F32)
        rank = jnp.dot(hit.astype(BF16), before, preferred_element_type=F32)
        slot = jnp.sum(
            hit * (rank + (lax.broadcasted_iota(I32, (places, cap), 0) * SLOT + 1).astype(F32)),
            axis=0, keepdims=True,
        ) - 1.0
        row_e = row_in[e : e + 1, :].astype(F32) + 1.0
        gate_e = gates_ref[e : e + 1, :]
        block = 4 * SLOT
        for b in range(places * SLOT // block):
            ids = (lax.broadcasted_iota(I32, (block, cap), 0) + b * block).astype(F32)
            here = ids == slot
            pick = jnp.sum(jnp.where(here, row_e, 0.0), axis=1, keepdims=True) - 1.0
            gate = jnp.sum(jnp.where(here, gate_e, 0.0), axis=1, keepdims=True)
            wide = jnp.broadcast_to(pick, (block, 128)).astype(BF16)
            picks_out[e, 4 * b : 4 * b + 4] = wide.reshape(4, SLOT, 128)
            gate_col[e, b * block : (b + 1) * block] = jnp.broadcast_to(gate, (block, 128))
    picks_in[:, 0] = picks_out[:, 0]

    pl.semaphore_wait(barrier, places - 1 + 2)

    order = [p for name in sends for p in range(*chunks[name][:2])]
    picks = {}
    for p in order:
        if p:
            picks[p] = remote(
                picks_out.at[:, p], picks_in.at[:, p], pick_s.at[p], pick_r.at[p], owner_of(p)
            )
            picks[p].start()

    for copy in loads[:n_q]:
        copy.wait()

    out_going = {}
    sem_ids = iter(range(y_s.shape[0]))
    started = []

    def send_y(src, dst, target):
        k = next(sem_ids)
        copy = remote(src, dst, y_s.at[k], y_r.at[k], {"hp": target})
        copy.start()
        started.append(copy)
        return copy

    state = {}
    returns = {}
    weights_ready = False

    for step, name in schedule:
        lo, hi, whole = chunks[name]
        n, m = hi - lo, (hi - lo) * SLOT
        rng = pl.ds(lo, n)
        if step == "X":
            for p in range(lo, hi):
                if p:
                    picks[p].wait_recv()
            token_id = lax.broadcasted_iota(I32, (m, 128), 1).astype(F32)
            for e in range(n_exp):
                want = picks_in[e, lo:hi].reshape(m, 128).astype(F32)
                parts = [
                    (token_id + float(128 * k) == want).astype(F32) for k in range(n_tok // 128)
                ]
                hot = jnp.concatenate(parts, axis=1).astype(BF16)
                onehot[e, lo:hi] = hot.reshape(n, SLOT, n_tok)

                def rows_of(q):
                    taken = jnp.dot(hot, tok[q], preferred_element_type=F32).astype(BF16)
                    pout[q, e, lo:hi] = taken.reshape(n, SLOT, feat)
                    if lo == 0:
                        chosen[q, e, 0] = taken[:SLOT]

                if whole:
                    pl.loop(0, n_q)(rows_of)
                else:
                    rows_of(y)
            for p in range(lo, hi):
                if p:
                    at = (slice(None), slice(None), p) if whole else (y, slice(None), p)
                    out_going[p] = remote(
                        pout.at[at], chosen.at[at], disp_s.at[p], disp_r.at[p], expert_of(p)
                    )
                    out_going[p].start()
        elif step == "G":
            for p in range(lo, hi):
                out_going[p].wait_recv()
            state[name, "G"] = [
                send_y(chosen.at[y, :, rng], chosen.at[y, :, rng], target) for target in (y_up, y_dn)
            ]
        elif step == "F":
            for copy in state[name, "G"]:
                copy.wait_recv()
            state[name, "F"] = [
                send_y(chosen.at[y_dn, 0, rng], chosen.at[y_dn, 0, rng], y_up),
                send_y(chosen.at[y_up, 1, rng], chosen.at[y_up, 1, rng], y_dn),
            ]
        elif step in "CE":
            e = "CE".index(step)
            if e == 0:
                for p in range(lo, hi):
                    if p and whole:
                        out_going[p].wait_recv()
                for p in range(lo, hi):
                    if p:
                        out_going[p].wait_send()
            if not weights_ready:
                for copy in loads[n_q:]:
                    copy.wait()
                weights_ready = True
            if not whole:
                state[name, "F"][e].wait_recv()
            total = jnp.zeros((m, 2 * hid), F32)
            for q in range(n_q):
                total += jnp.dot(
                    chosen[q, e, lo:hi].reshape(m, feat),
                    wgu[e, q * feat : (q + 1) * feat, :],
                    preferred_element_type=F32,
                )
            gate, up = total[:, :hid], total[:, hid:]
            hidden = (gate / (1.0 + jnp.exp(-gate)) * up).astype(BF16)
            weight = gate_col[e, lo * SLOT : hi * SLOT][:, :1]

            @pl.loop(0, n_q)
            def _(q):
                value = jnp.dot(hidden, wd[e, q], preferred_element_type=F32) * weight
                pout[q, e, lo:hi] = value.astype(BF16).reshape(n, SLOT, feat)

            ahead, behind = (y_up, y_dn) if e == 0 else (y_dn, y_up)
            state[name, "V", e] = send_y(pout.at[y_far, e, rng], via.at[e, rng], ahead)
            state[name, "D", e] = send_y(pout.at[behind, e, rng], fin.at[1 - e, e, rng], behind)
        elif step in "AB":
            e = "AB".index(step)
            ahead = (y_up, y_dn)[e]
            state[name, "V", e].wait_recv()
            pout[ahead, e, lo:hi] = (
                pout[ahead, e, lo:hi].astype(F32) + via[e, lo:hi].astype(F32)
            ).astype(BF16)
            state[name, "S", e] = send_y(pout.at[ahead, e, rng], fin.at[e, e, rng], ahead)
        elif step == "T":
            for e in range(n_exp):
                state[name, "D", e].wait_recv()
                state[name, "S", e].wait_recv()
                back[e, lo:hi] = (
                    pout[y, e, lo:hi].astype(F32)
                    + fin[0, e, lo:hi].astype(F32)
                    + fin[1, e, lo:hi].astype(F32)
                ).astype(BF16)
            for p in range(lo, hi):
                if p:
                    returns[p] = remote(
                        back.at[:, p], ret.at[:, p], ret_s.at[p], ret_r.at[p], owner_of(p)
                    )
                    returns[p].start()
                else:
                    ret[:, 0] = back[:, 0]
        else:
            for p in range(lo, hi):
                if p:
                    returns[p].wait_recv()
            total = None
            for e in range(n_exp):
                value = lax.dot_general(
                    onehot[e, lo:hi].reshape(m, n_tok),
                    ret[e, lo:hi].reshape(m, feat),
                    (((0,), (0,)), ((), ())),
                    preferred_element_type=F32,
                )
                total = value if total is None else total + value
            merged = [w for s, w in schedule if s == "M"]
            if name != merged[0]:
                total = total + acc[...]
            if name == merged[-1]:
                out_ref[...] = total.astype(BF16)
            else:
                acc[...] = total

    for copy in [*picks.values(), *returns.values(), *started]:
        copy.wait_send()


def per_device(tokens, expert_rows, expert_counts, choice_gates, gate_proj, up_proj, down_proj):
    groups = lax.axis_size("ep")
    n_q = lax.axis_size("hp")
    n_tok, width = tokens.shape
    n_exp, cap = expert_rows.shape
    hid = gate_proj.shape[2]
    feat = width // n_q
    chunks = plan(groups)[2]
    hops = sum(6 if whole else 10 for _, _, whole in chunks.values())
    any_space = pl.BlockSpec(memory_space=pl.ANY)
    vmem = pl.BlockSpec(memory_space=pltpu.VMEM)
    dma = pltpu.SemaphoreType.DMA
    full = (n_q, n_exp, groups, SLOT, feat)
    return pl.pallas_call(
        functools.partial(kernel, groups, n_q),
        out_shape=jax.ShapeDtypeStruct((n_tok, feat), BF16),
        in_specs=[vmem, pl.BlockSpec(memory_space=pltpu.SMEM), vmem, any_space, any_space, any_space, any_space],
        out_specs=vmem,
        scratch_shapes=[
            pltpu.VMEM((n_q, n_tok, feat), BF16),
            pltpu.VMEM((n_exp, width, 2 * hid), BF16),
            pltpu.VMEM((n_exp, n_q, hid, feat), BF16),
            pltpu.VMEM(full, BF16),
            pltpu.VMEM(full, BF16),
            pltpu.VMEM((2, groups, SLOT, feat), BF16),
            pltpu.VMEM((2, n_exp, groups, SLOT, feat), BF16),
            pltpu.VMEM((n_exp, groups, SLOT, feat), BF16),
            pltpu.VMEM((n_exp, groups, SLOT, feat), BF16),
            pltpu.VMEM((n_exp, groups, SLOT, n_tok), BF16),
            pltpu.VMEM((n_tok, feat), F32),
            pltpu.VMEM((n_exp, groups, SLOT, 128), BF16),
            pltpu.VMEM((n_exp, groups, SLOT, 128), BF16),
            pltpu.VMEM((n_exp, groups * SLOT, 128), F32),
            dma((n_q + n_exp * (2 + n_q),)),
            dma((groups,)),
            dma((groups,)),
            dma((groups,)),
            dma((groups,)),
            dma((groups,)),
            dma((groups,)),
            dma((hops,)),
            dma((hops,)),
        ],
        compiler_params=pltpu.CompilerParams(
            collective_id=0, has_side_effects=True, vmem_limit_bytes=60 * 1024 * 1024
        ),
        cost_estimate=pl.CostEstimate(
            flops=6 * n_exp * cap * width * hid, bytes_accessed=24 * 1024 * 1024, transcendentals=0
        ),
    )(
        expert_rows, expert_counts, choice_gates,
        tokens, gate_proj, up_proj, down_proj,
    )


def solution(mesh):
    return jax.shard_map(
        per_device,
        mesh=mesh,
        in_specs=(
            P("ep", None),
            P("ep", None),
            P("ep"),
            P("ep", None),
            P("ep", None, "hp"),
            P("ep", None, "hp"),
            P("ep", "hp", None),
        ),
        out_specs=P("ep", "hp"),
        check_vma=False,
    )
```
